32 devices in a mesh: row: 4 (over z), col: 4 (over y, core), rep: 2 (over x).
Axes of the slice: x: 2, y: 2, z: 4, core: 2. Of those that a mesh axis runs over, the one named last changes fastest.
Arguments:
- hidden: bfloat16 [2, 2048, 2048], P('rep', ('row', 'col')), may hold values from -6 to 6
- lengths: int32 [2, 4], P('rep'), may hold values from 1 to 1536, 2048 in all within a row
- prefix_latent: bfloat16 [512, 576], P(('row', 'col', 'rep')), may hold values from -6 to 6
- gain_in: bfloat16 [2048], replicated, may hold values from 0.25 to 1.75
- query_weight: bfloat16 [2048, 1536], replicated, may hold values from -0.125 to 0.125
- latent_down: bfloat16 [2048, 576], replicated, may hold values from -0.125 to 0.125
- latent_gain: bfloat16 [512], replicated, may hold values from 0.25 to 1.75
- key_absorb: bfloat16 [8, 128, 512], replicated, may hold values from -8 to 8
- value_up: bfloat16 [8, 512, 128], replicated, may hold values from -0.25 to 0.25
- output_weight: bfloat16 [1024, 2048], replicated, may hold values from -0.5 to 0.5
- post_gain: bfloat16 [2048], replicated, may hold values from 0.25 to 1.75
- routes: int32 [2, 2048, 6], P('rep', ('row', 'col')), may hold values from 0 to 63, all different within a row; in each aligned block of 128 rows (0 to 127, 128 to 255, ..., all dimensions but the last counted through in order) at most 16 rows name the same one
- gate_weights: float32 [2, 2048, 6], P('rep', ('row', 'col')), may hold values from 0.1 to 1
- expert_gate_up: bfloat16 [128, 2048, 1408], P(('row', 'col', 'rep')), may hold values from -0.125 to 0.125
- expert_down: bfloat16 [128, 704, 2048], P(('row', 'col', 'rep')), may hold values from -0.15625 to 0.15625
Outputs:
- attended: bfloat16 [2, 2048, 2048], P('rep', ('row', 'col'))
- layer_out: bfloat16 [2, 2048, 2048], P('rep', ('row', 'col'))
The draws below stay inside these ranges and needn't reach their ends.
Inputs may be any that keep to these rules, and one draw needn't show every extreme that they name: In each group the 4 lengths sum to 2048, and one of them is exactly 1536. `routes`: A token's 6 experts differ; among the 128 tokens of one device (aligned blocks of 128 tokens of a group) no expert is chosen more than 16 times, a bound that some block reaches.
All inputs are finite; a program needn't handle non-finite values.
Results may differ from the reference program's by a relative error of at most 0.014.
The reference program's roundings to bfloat16 on the way count: a program that leaves them out, or rounds other values in their place, can miss the bound.
Values may be sent and summed in bfloat16 or wider, within the bound.
A program may use at most 128 MiB of HBM per device.

```python
import math
import jax
import jax.numpy as jnp
import numpy as np
from jax import lax

D = 2048
H = 8
NOPE = 128
ROPE = 64
RANK = 512
VD = 128
E = 64
TOP = 6
FF = 1408
FH = 704
REQS = 4
TOK_DEV = 128
TG = 2048
P_SIZE = 512
CAP = 16
N_REP = 2


def draw_key_absorb(key, part):
    base = jax.random.normal(jax.random.fold_in(key, 11), (H, NOPE, RANK), jnp.float32)
    scale_value = 3.0 / math.sqrt(RANK)
    return jnp.clip(base * scale_value, -8.0, 8.0).astype(jnp.bfloat16)


def block_scale(own_key, shape, pieces, low, top_value):
    gain, own = 1.0, jax.random.fold_in(own_key, 6)
    for position, shards_of in pieces:
        steps = jnp.exp(jax.random.uniform(jax.random.fold_in(own, position), (shards_of,), jnp.float32, low / len(pieces), top_value / len(pieces)))
        gain = gain * jnp.repeat(steps, shape[position] // shards_of).reshape([-1 if axis == position else 1 for axis in range(len(shape))])
    return gain


def split_up(amount, total, most, lean):
    portions = [(1 << 20) // math.isqrt(standing ** lean) + 1 for standing in range(2, amount + 1)]
    spare, counts = total - most - (amount - 1), [1] * (amount - 1)
    while spare > 0:
        free = [i for i in range(amount - 1) if counts[i] < most]
        mass, remaining = sum([portions[i] for i in free]), spare
        for i in free:
            more = min(most - counts[i], max(1, remaining * portions[i] // mass), spare)
            counts[i] = counts[i] + more
            spare = spare - more
    return np.array([most] + counts)


def ragged_sizes(stream_key, amount, total, reach, slope):
    if amount == 2:
        one = jax.random.randint(stream_key, (), max(1, total - reach), min(reach, total - 1) + 1)
        return jnp.stack([one, total - one])
    tallies = jnp.asarray(split_up(amount, total, reach, slope), jnp.int32)
    twos = (amount - 1) // 2
    donor, sink = tallies[1:1 + 2 * twos:2], tallies[2:2 + 2 * twos:2]
    room = jnp.minimum(donor - 1, reach - sink)
    moved = jax.random.randint(jax.random.fold_in(stream_key, 1), (twos,), 0, 1 << 20) % (room + 1)
    tallies = tallies.at[1:1 + 2 * twos:2].set(donor - moved).at[2:2 + 2 * twos:2].set(sink + moved)
    return tallies[jax.random.permutation(jax.random.fold_in(stream_key, 2), amount)]


def shared_out(rng, own, number, rows, amount, top, reach, lean):
    sequence = jax.random.permutation(rng, amount)
    heavy_load, common = load_shares(amount, rows * top, reach, lean, True), load_shares(amount, rows * top, reach, lean, False)
    places = jnp.arange(amount)

    def named(tallies, offset_by):
        used = int((tallies > 0).sum())
        fixed = max(1, used // 4)
        shifted = fixed + (places - fixed + offset_by * (used - fixed)) % max(1, amount - fixed)
        return jnp.zeros((amount,), jnp.int32).at[sequence[jnp.where(places < fixed, places, shifted)]].set(jnp.asarray(tallies, jnp.int32))

    tallies = jnp.where(number % 4 == 0, named(heavy_load, number // 4), named(common, number - number // 4 - 1))
    mixed = jax.random.permutation(jax.random.fold_in(own, 3), amount)
    giver, taker = mixed[0:amount // 2 * 2:2], mixed[1:amount // 2 * 2:2]
    slack = jnp.minimum(tallies[giver] - 1, reach - tallies[taker]) // 2
    slack = jnp.where((giver == sequence[0]) | (taker == sequence[0]) | (tallies[taker] == 0), 0, jnp.maximum(slack, 0))
    shifted = jax.random.randint(jax.random.fold_in(own, 4), (amount // 2,), 0, 1 << 20) % (slack + 1)
    tallies = tallies.at[giver].add(-shifted).at[taker].add(shifted)
    labels = jnp.searchsorted(jnp.cumsum(tallies), jnp.arange(rows * top), side="right").astype(jnp.int32)
    grid = labels.reshape(top, rows).T
    grid = grid[jax.random.permutation(jax.random.fold_in(own, 1), rows)]
    offset_by = jax.random.randint(jax.random.fold_in(own, 2), (rows, 1), 0, top)
    return jnp.take_along_axis(grid, (jnp.arange(top)[None, :] + offset_by) % top, axis=1)


def load_shares(count, total, bound, lean, full):
    portions = [(1 << 20) // math.isqrt(rank ** lean) + 1 for rank in range(1, count + 1)]
    largest = bound if full else min(bound, max(-(-total // count), total * portions[0] // sum(portions)))
    least = 1 if total - largest >= count - 1 else 0
    counts, surplus = [largest] + [least] * (count - 1), total - largest - least * (count - 1)
    while surplus > 0:
        candidates = [i for i in range(1, count) if counts[i] < largest] or [i for i in range(1, count) if counts[i] < bound]
        whole, remaining = sum([portions[i] for i in candidates]), surplus
        for i in candidates:
            addition = min(bound - counts[i], max(1, remaining * portions[i] // whole), surplus)
            counts[i] = counts[i] + addition
            surplus = surplus - addition
    return np.array(counts)


def noise(stream_key, extent, width, bound, split=(), kind=jnp.bfloat16):
    values = jax.random.normal(stream_key, extent, jnp.float32) * width
    if len(split) > 0:
        values = block_scale(stream_key, extent, split, -0.22, 0.18) * values
    return jnp.clip(values, min=-bound, max=bound).astype(kind)


def setup_inputs(seed: int = 0) -> dict:
    streams_of = jax.random.split(jax.random.key(seed), 16)
    hidden = noise(streams_of[0], (N_REP, TG, D), 1.0, 6.0, ((0, 2), (1, 16)))
    lengths = jax.vmap(lambda own: ragged_sizes(own, REQS, TG, 3 * TG // 4, 2))(jax.random.split(streams_of[1], N_REP)).reshape((N_REP, REQS)).astype(jnp.int32)
    prefix_latent = noise(streams_of[2], (P_SIZE, RANK + ROPE), 1.0, 6.0, ((0, 32),))
    gain_in = jnp.clip(1.0 + 0.15 * jax.random.normal(streams_of[3], (D,), jnp.float32), 0.25, 1.75).astype(jnp.bfloat16)
    query_weight = noise(streams_of[4], (D, H * (NOPE + ROPE)), D ** -0.5, 0.125)
    latent_down = noise(streams_of[5], (D, RANK + ROPE), D ** -0.5, 0.125)
    latent_gain = jnp.clip(1.0 + 0.15 * jax.random.normal(streams_of[6], (RANK,), jnp.float32), 0.25, 1.75).astype(jnp.bfloat16)
    key_absorb = draw_key_absorb(jax.random.fold_in(streams_of[15], 71), 0)
    value_up = noise(streams_of[8], (H, RANK, VD), RANK ** -0.5, 0.25)
    output_weight = noise(streams_of[9], (H * VD, D), (H * VD // 8) ** -0.5, 0.5)
    post_gain = jnp.clip(1.0 + 0.15 * jax.random.normal(streams_of[10], (D,), jnp.float32), 0.25, 1.75).astype(jnp.bfloat16)
    routes_keys = jax.random.split(jax.random.fold_in(streams_of[11], 1), N_REP * TG // TOK_DEV)
    routes_turns = jax.random.permutation(jax.random.fold_in(streams_of[11], 3), N_REP * TG // TOK_DEV)
    routes = jax.vmap(lambda own, number: shared_out(jax.random.fold_in(streams_of[11], 2), own, number, TOK_DEV, E, TOP, CAP, 1))(routes_keys, routes_turns).reshape((N_REP, TG, TOP))
    gate_weights = jnp.clip(jnp.exp(math.log(1.0) - 2.3025851 * jax.random.uniform(streams_of[12], (N_REP, TG, TOP), jnp.float32) ** block_scale(streams_of[12], (N_REP, TG, TOP), ((0, 2), (1, 16)), -0.2, 0.2)), 0.1, 1.0)
    expert_gate_up = noise(streams_of[13], (2 * E, D, 2 * FH), D ** -0.5, 0.125, ((0, 32),))
    expert_down = noise(streams_of[14], (2 * E, FH, D), FF ** -0.5, 0.15625, ((0, 32),))
    return dict(hidden=hidden, lengths=lengths, prefix_latent=prefix_latent, gain_in=gain_in, query_weight=query_weight, latent_down=latent_down, latent_gain=latent_gain, key_absorb=key_absorb, value_up=value_up, output_weight=output_weight, post_gain=post_gain, routes=routes, gate_weights=gate_weights, expert_gate_up=expert_gate_up, expert_down=expert_down)


epsilon = 1e-06
rope_base = 50000.0

def rounded(values):
    return lax.optimization_barrier(values.astype(jnp.bfloat16))

def rms_scale(values, gain_vector):
    mean_square = lax.optimization_barrier(jnp.mean(values * values, axis=-1, keepdims=True))
    return values * lax.rsqrt(mean_square + epsilon) * gain_vector.astype(jnp.float32)

def rope_tables(positions, rope_width):
    halfway = rope_width // 2
    frequency = jnp.power(rope_base, -2.0 * jnp.arange(halfway, dtype=jnp.float32) / rope_width)
    angles = positions.astype(jnp.float32)[:, None] * frequency[None, :]
    return (jnp.cos(angles), jnp.sin(angles))

def rotate(values, cosine, sine_table):
    halfway = values.shape[-1] // 2
    leading = values[..., :halfway]
    trailing = values[..., halfway:]
    return jnp.concatenate([leading * cosine - trailing * sine_table, trailing * cosine + leading * sine_table], axis=-1)

def token_layout(group_lengths, first_place, row_count):
    ends = jnp.cumsum(group_lengths).astype(jnp.int32)
    starts = (ends - group_lengths).astype(jnp.int32)
    places = (first_place + jnp.arange(row_count, dtype=jnp.int32)).astype(jnp.int32)
    member = lax.optimization_barrier(jnp.sum((places[:, None] >= ends[None, :]).astype(jnp.int32), axis=1)).astype(jnp.int32)
    chosen = member[:, None] == jnp.arange(group_lengths.shape[0], dtype=jnp.int32)[None, :]
    offsets = lax.optimization_barrier(jnp.sum(jnp.where(chosen, starts[None, :], 0), axis=1)).astype(jnp.int32)
    return (member, places, (places - offsets).astype(jnp.int32))

def make_queries(normed, positions, query_weight, latent_down, latent_gain, key_absorb):
    row_count = normed.shape[0]
    head_count = key_absorb.shape[0]
    plain_width = key_absorb.shape[1]
    latent_width = latent_gain.shape[0]
    projected = jnp.dot(normed, query_weight, preferred_element_type=jnp.float32).reshape(row_count, head_count, -1)
    rope_width = projected.shape[-1] - plain_width
    cosine, sine_table = rope_tables(positions, rope_width)
    query_plain = rounded(projected[..., :plain_width]).astype(jnp.float32)
    query_rotary = rotate(projected[..., plain_width:], cosine[:, None, :], sine_table[:, None, :]).astype(jnp.bfloat16)
    query_latent = jnp.einsum('thn,hnr->thr', query_plain, key_absorb.astype(jnp.float32)).astype(jnp.bfloat16)
    query_rows = jnp.concatenate([query_latent, query_rotary], axis=-1)
    compressed = jnp.dot(normed, latent_down, preferred_element_type=jnp.float32)
    latent = rms_scale(compressed[:, :latent_width], latent_gain)
    key_rotary = rotate(compressed[:, latent_width:], cosine, sine_table)
    key_rows = jnp.concatenate([latent, key_rotary], axis=-1).astype(jnp.bfloat16)
    return (query_rows, key_rows)

def reference(hidden, lengths, prefix_latent, gain_in, query_weight, latent_down, latent_gain, key_absorb, value_up, output_weight, post_gain, routes, gate_weights, expert_gate_up, expert_down):
    scale_factor = 1.0 / math.sqrt(NOPE + ROPE)
    prefix_rows = prefix_latent.shape[0]

    def group_attention(inputs):
        group_hidden, group_lengths = inputs
        member, places, offsets = token_layout(group_lengths, 0, TG)
        normed = rms_scale(group_hidden.astype(jnp.float32), gain_in).astype(jnp.bfloat16)
        query_rows, key_rows = make_queries(normed, prefix_rows + offsets, query_weight, latent_down, latent_gain, key_absorb)
        all_keys = jnp.concatenate([prefix_latent, key_rows], axis=0)
        scores = jnp.einsum('thc,kc->thk', query_rows.astype(jnp.float32), all_keys.astype(jnp.float32)) * scale_factor
        allowed = (member[:, None] == member[None, :]) & (places[:, None] >= places[None, :])
        allowed = jnp.concatenate([jnp.ones((TG, prefix_rows), dtype=jnp.bool_), allowed], axis=1)
        scores = jnp.where(allowed[:, None, :], scores, -jnp.inf)
        peak = lax.optimization_barrier(jnp.max(scores, axis=2, keepdims=True))
        weights = jnp.exp(scores - peak)
        normalizer = lax.optimization_barrier(jnp.sum(weights, axis=2, keepdims=True))
        weights_low = rounded(weights).astype(jnp.float32)
        mixed = jnp.einsum('thk,kr->thr', weights_low, all_keys[:, :RANK].astype(jnp.float32)) / normalizer
        head_values = jnp.einsum('thr,hrv->thv', rounded(mixed).astype(jnp.float32), value_up.astype(jnp.float32))
        joined = head_values.astype(jnp.bfloat16).reshape(TG, -1)
        return jnp.dot(joined, output_weight, preferred_element_type=jnp.float32)
    attention = lax.map(group_attention, (hidden, lengths))
    tokens_all = N_REP * TG
    block_count = tokens_all // TOK_DEV
    residual = (hidden.astype(jnp.float32) + attention).astype(jnp.bfloat16).reshape(tokens_all, D)
    normed_post = rms_scale(residual.astype(jnp.float32), post_gain).astype(jnp.bfloat16)
    choices_flat = routes.reshape(block_count, TOK_DEV * TOP)
    gate_flat = gate_weights.reshape(block_count, TOK_DEV * TOP)
    selected = (choices_flat[:, :, None] == jnp.arange(E, dtype=jnp.int32)[None, None, :]).astype(jnp.int32)
    slot_index = (lax.optimization_barrier(jnp.sum(jnp.cumsum(selected, axis=1) * selected, axis=2)) - 1).astype(jnp.int32)
    block_index = jnp.broadcast_to(jnp.arange(block_count, dtype=jnp.int32)[:, None], choices_flat.shape)
    token_index = (block_index * TOK_DEV + jnp.arange(TOK_DEV * TOP, dtype=jnp.int32)[None, :] // TOP).astype(jnp.int32)
    slot_table = jnp.full((block_count, E, CAP), tokens_all, jnp.int32).at[block_index, choices_flat, slot_index].set(token_index)
    gate_table = jnp.zeros((block_count, E, CAP), jnp.float32).at[block_index, choices_flat, slot_index].set(gate_flat)
    slot_table = jnp.transpose(slot_table, (1, 0, 2)).reshape(E, block_count * CAP)
    gate_table = jnp.transpose(gate_table, (1, 0, 2)).reshape(E, block_count * CAP)
    padded = jnp.concatenate([normed_post, jnp.zeros((1, D), jnp.bfloat16)], axis=0)

    def expert_step(mixture, inputs):
        gate_up_pair, down_pair, row_index, row_gates = inputs
        token_rows = jnp.take(padded, row_index, axis=0)
        outputs = []
        for half_index in range(2):
            joint = jnp.dot(token_rows, gate_up_pair[half_index], preferred_element_type=jnp.float32)
            active = (jax.nn.silu(joint[:, :FH]) * joint[:, FH:]).astype(jnp.bfloat16)
            outputs.append(rounded(jnp.dot(active, down_pair[half_index], preferred_element_type=jnp.float32)).astype(jnp.float32))
        combined = (outputs[0] + outputs[1]) * row_gates[:, None]
        return (mixture.at[row_index].add(combined, mode='drop'), None)
    mixture = lax.scan(expert_step, jnp.zeros((tokens_all, D), jnp.float32), (expert_gate_up.reshape(E, 2, D, 2 * FH), expert_down.reshape(E, 2, FH, D), slot_table, gate_table))[0]
    layer_out = (residual.astype(jnp.float32) + mixture).astype(jnp.bfloat16).reshape(N_REP, TG, D)
    return (attention.astype(jnp.bfloat16), layer_out)
```

```python
import jax
import jax.numpy as jnp
import functools
from jax import lax
from jax.experimental import pallas as pl
from jax.experimental.pallas import tpu as pltpu
from jax.sharding import PartitionSpec as P

E = 64
CAP = 16


epsilon = 1e-06
rope_base = 50000.0


def rms_scale(values, gain_vector):
    mean_square = jnp.mean(values * values, axis=-1, keepdims=True)
    return values * lax.rsqrt(mean_square + epsilon) * gain_vector.astype(jnp.float32)


def rope_tables(positions, rope_width):
    halfway = rope_width // 2
    frequency = jnp.power(rope_base, -2.0 * jnp.arange(halfway, dtype=jnp.float32) / rope_width)
    angles = positions.astype(jnp.float32)[:, None] * frequency[None, :]
    return (jnp.cos(angles), jnp.sin(angles))


def rotate(values, cosine, sine_table):
    halfway = values.shape[-1] // 2
    leading = values[..., :halfway]
    trailing = values[..., halfway:]
    return jnp.concatenate(
        [leading * cosine - trailing * sine_table, trailing * cosine + leading * sine_table],
        axis=-1,
    )


def make_queries(normed, positions, query_weight, latent_down, latent_gain, key_absorb):
    row_count = normed.shape[0]
    head_count = key_absorb.shape[0]
    plain_width = key_absorb.shape[1]
    latent_width = latent_gain.shape[0]
    projected = jnp.dot(normed, query_weight, preferred_element_type=jnp.float32).reshape(
        row_count, head_count, -1
    )
    rope_width = projected.shape[-1] - plain_width
    cosine, sine_table = rope_tables(positions, rope_width)
    query_plain = projected[..., :plain_width].astype(jnp.bfloat16)
    query_rotary = rotate(
        projected[..., plain_width:], cosine[:, None, :], sine_table[:, None, :]
    ).astype(jnp.bfloat16)
    query_latent = jnp.einsum(
        "thn,hnr->thr", query_plain, key_absorb, preferred_element_type=jnp.float32
    ).astype(jnp.bfloat16)
    query_rows = jnp.concatenate([query_latent, query_rotary], axis=-1)
    compressed = jnp.dot(normed, latent_down, preferred_element_type=jnp.float32)
    latent = rms_scale(compressed[:, :latent_width], latent_gain)
    key_rotary = rotate(compressed[:, latent_width:], cosine, sine_table)
    key_rows = jnp.concatenate([latent, key_rotary], axis=-1).astype(jnp.bfloat16)
    return (query_rows, key_rows)


MESH = pl.DeviceIdType.MESH
VMEM_BYTES = 48 * 1024 * 1024


def position():
    return lax.axis_index("row"), lax.axis_index("col"), lax.axis_index("rep")


def greet(peers):
    barrier = pltpu.get_barrier_semaphore()
    for peer in peers:
        pl.semaphore_signal(barrier, inc=1, device_id=peer, device_id_type=MESH)
    pl.semaphore_wait(barrier, len(peers))


def remote(source, target, send, recv, peer):
    return pltpu.make_async_remote_copy(
        src_ref=source,
        dst_ref=target,
        send_sem=send,
        recv_sem=recv,
        device_id=peer,
        device_id_type=MESH,
    )


def gather_kernel(sizes, kv_ref, prefix_ref, out_ref, local, rep_sems, row_sems, col_sems):
    rows, cols, reps = sizes
    row, col, rep = position()
    tokens, shard = kv_ref.shape[0], prefix_ref.shape[0]
    strides = []
    stride = cols // 2
    while stride:
        strides.append(stride)
        stride //= 2

    def across(index, stride):
        return index + stride * (1 - 2 * (lax.div(index, stride) % 2))

    rep_peers = [(row, col, lax.rem(rep + d, reps)) for d in range(1, reps)]
    row_peers = [(lax.rem(row + d, rows), col, rep) for d in range(1, rows)]
    col_peers = [(row, across(col, s), rep) for s in strides]
    greet(rep_peers + row_peers + col_peers)
    mine = out_ref.at[row, col, pl.ds(tokens + rep * shard, shard)]
    pending = []
    keep = [
        pltpu.make_async_copy(kv_ref, out_ref.at[row, col, pl.ds(0, tokens)], local.at[0]),
        pltpu.make_async_copy(prefix_ref, mine, local.at[1]),
    ]
    early = [
        remote(prefix_ref, mine, rep_sems.at[0, d], rep_sems.at[1, d], peer)
        for d, peer in enumerate(rep_peers)
    ]
    for copy in early + keep:
        copy.start()
    for copy in keep:
        copy.wait()
    for copy in early:
        copy.wait()
    own = out_ref.at[row, col]
    arrivals = [None]
    for d, peer in enumerate(row_peers):
        copy = remote(own, own, row_sems.at[0, d], row_sems.at[1, d], peer)
        copy.start()
        arrivals.append(copy)
    sent = {}

    def forward(step, d, m, held_col):
        block = out_ref.at[lax.rem(row + rows - d, rows), held_col]
        copy = remote(
            block, block, col_sems.at[0, step, d, m], col_sems.at[1, step, d, m], col_peers[step]
        )
        copy.start()
        sent[step, d, m] = copy

    for d in range(rows):
        if d:
            arrivals[d].wait_recv()
        for step in range(len(strides)):
            forward(step, d, 0, col)
    held = [col]
    for step, stride in enumerate(strides):
        fresh = [across(c, stride) for c in held]
        for d in range(rows):
            for m, c in enumerate(fresh):
                sent[step, d, m].wait_recv()
                for later in range(step + 1, len(strides)):
                    forward(later, d, len(held) + m, c)
        held = held + fresh
    for copy in arrivals[1:]:
        copy.wait_send()
    for copy in sent.values():
        copy.wait_send()


def gather_keys(key_rows, prefix_latent):
    rows, cols, reps = (lax.axis_size(name) for name in ("row", "col", "rep"))
    shard, width = prefix_latent.shape
    steps = max(1, cols.bit_length() - 1)
    return pl.pallas_call(
        functools.partial(gather_kernel, (rows, cols, reps)),
        out_shape=jax.ShapeDtypeStruct(
            (rows, cols, key_rows.shape[0] + reps * shard, width), jnp.bfloat16
        ),
        in_specs=[pl.BlockSpec(memory_space=pltpu.VMEM)] * 2,
        out_specs=pl.BlockSpec(memory_space=pl.ANY),
        scratch_shapes=[
            pltpu.SemaphoreType.DMA((2,)),
            pltpu.SemaphoreType.DMA((2, reps)),
            pltpu.SemaphoreType.DMA((2, rows)),
            pltpu.SemaphoreType.DMA((2, steps, rows, cols)),
        ],
        compiler_params=pltpu.CompilerParams(collective_id=0, has_side_effects=True),
    )(key_rows, prefix_latent)


def plane_peers(sizes):
    rows, cols, reps = sizes
    row, col, rep = position()
    plane = cols * reps
    me = col * reps + rep
    others = [lax.rem(me + k, plane) for k in range(1, plane)]
    peers = [(row, lax.div(q, reps), lax.rem(q, reps)) for q in others]
    down = [(lax.rem(row + d, rows), col, rep) for d in range(1, rows)]
    return row, me, others, peers, down


def turns(rows):
    return sorted(range(rows), key=lambda d: (min(d, rows - d), d))


def dispatch_kernel(
    sizes, x_ref, tab_ref, out_ref, tabs_ref, xbuf, tbuf, rbuf, local, xsem, tsem, psem
):
    rows, cols, reps = sizes
    row, me, others, peers, down = plane_peers(sizes)
    tokens, width = x_ref.shape
    held = out_ref.shape[0]
    slots = tab_ref.shape[2]
    greet(peers + down)
    streams = [None]
    for d in range(1, rows):
        peer = down[d - 1]
        table = remote(tab_ref.at[peer[0]], tbuf.at[d], tsem.at[0, d], tsem.at[1, d], peer)
        block = remote(x_ref, xbuf.at[d], xsem.at[0, d], xsem.at[1, d], peer)
        table.start()
        block.start()
        streams.append((table, block))
    tabs_ref[0] = tab_ref[row]
    place = lax.broadcasted_iota(jnp.int32, (tokens, slots), 0).astype(jnp.float32)
    tile = min(width, 512)
    waiting = []
    for d in turns(rows):
        if d:
            streams[d][0].wait_recv()
            streams[d][1].wait_recv()
            tabs_ref[d] = tbuf[d]
        table = tabs_ref[d]
        onehot = jnp.where(place == table[0:1, :], 1.0, 0.0).astype(jnp.bfloat16)
        for start in range(0, width, tile):
            part = x_ref[:, start : start + tile] if d == 0 else xbuf[d, :, start : start + tile]
            picked = lax.dot_general(
                onehot, part, (((0,), (0,)), ((), ())), preferred_element_type=jnp.float32
            ).astype(jnp.bfloat16)
            rbuf[d, :, :, :, start : start + tile] = picked.reshape(-1, held, CAP, tile)
        origin = lax.rem(row + rows - d, rows)
        target = out_ref.at[:, origin, me]
        for k, (q, peer) in enumerate(zip(others, peers)):
            copy = remote(rbuf.at[d, q], target, psem.at[0, d, k], psem.at[1, d, k], peer)
            copy.start()
            waiting.append(copy)
        copy = pltpu.make_async_copy(rbuf.at[d, me], target, local.at[d])
        copy.start()
        waiting.append(copy)
    for d in range(1, rows):
        streams[d][0].wait_send()
        streams[d][1].wait_send()
    for copy in waiting:
        copy.wait()


def dispatch(normed, tables, per_device):
    rows, cols, reps = (lax.axis_size(name) for name in ("row", "col", "rep"))
    tokens, width = normed.shape
    slots = tables.shape[2]
    plane = cols * reps
    held = max(1, per_device // 2)
    vmem = pl.BlockSpec(memory_space=pltpu.VMEM)
    return pl.pallas_call(
        functools.partial(dispatch_kernel, (rows, cols, reps)),
        out_shape=(
            jax.ShapeDtypeStruct((held, rows, plane, CAP, width), jnp.bfloat16),
            jax.ShapeDtypeStruct(tables.shape, jnp.float32),
        ),
        in_specs=[vmem, vmem],
        out_specs=(pl.BlockSpec(memory_space=pl.ANY), vmem),
        scratch_shapes=[
            pltpu.VMEM((rows, tokens, width), jnp.bfloat16),
            pltpu.VMEM((rows, 8, slots), jnp.float32),
            pltpu.VMEM((rows, plane, held, CAP, width), jnp.bfloat16),
            pltpu.SemaphoreType.DMA((rows,)),
            pltpu.SemaphoreType.DMA((2, rows)),
            pltpu.SemaphoreType.DMA((2, rows)),
            pltpu.SemaphoreType.DMA((2, rows, plane)),
        ],
        compiler_params=pltpu.CompilerParams(
            collective_id=1, has_side_effects=True, vmem_limit_bytes=VMEM_BYTES
        ),
    )(normed, tables)


def combine_kernel(
    sizes, y_ref, tabs_ref, residual_ref, out_ref, ybuf, sums, pbuf, total, local, psem, rsem
):
    rows, cols, reps = sizes
    row, me, others, peers, down = plane_peers(sizes)
    tokens, width = residual_ref.shape
    slots = tabs_ref.shape[2]
    greet(peers + down)
    order = turns(rows)[::-1]
    waiting = {}
    for d in order:
        origin = lax.rem(row + rows - d, rows)
        waiting[d] = []
        for k, (q, peer) in enumerate(zip(others, peers)):
            copy = remote(
                y_ref.at[:, origin, q], ybuf.at[d, me], psem.at[0, d, k], psem.at[1, d, k], peer
            )
            copy.start()
            waiting[d].append(copy)
        copy = pltpu.make_async_copy(y_ref.at[:, origin, me], ybuf.at[d, me], local.at[d])
        copy.start()
        waiting[d].append(copy)
    place = lax.broadcasted_iota(jnp.int32, (tokens, slots), 0).astype(jnp.float32)
    tile = min(width, 512)
    back = []
    for d in order:
        for copy in waiting[d]:
            copy.wait()
        table = tabs_ref[d]
        gates = jnp.where(place == table[0:1, :], table[1:2, :], 0.0)
        coarse = gates.astype(jnp.bfloat16)
        fine = (gates - coarse.astype(jnp.float32)).astype(jnp.bfloat16)
        for start in range(0, width, tile):
            part = ybuf[d, :, :, :, start : start + tile].reshape(slots, tile)
            mixture = jnp.dot(coarse, part, preferred_element_type=jnp.float32) + jnp.dot(
                fine, part, preferred_element_type=jnp.float32
            )
            if d == 0:
                total[:, start : start + tile] = mixture
            else:
                sums[d, :, start : start + tile] = mixture.astype(jnp.bfloat16)
        if d:
            copy = remote(
                sums.at[d], pbuf.at[d], rsem.at[0, d], rsem.at[1, d], down[rows - d - 1]
            )
            copy.start()
            back.append((d, copy))
    for d, copy in back:
        copy.wait()
        total[...] += pbuf[d].astype(jnp.float32)
    out_ref[...] = (residual_ref[...].astype(jnp.float32) + total[...]).astype(jnp.bfloat16)


def combine(produced, tables, residual):
    rows, cols, reps = (lax.axis_size(name) for name in ("row", "col", "rep"))
    tokens, width = residual.shape
    held, plane = produced.shape[0], cols * reps
    vmem = pl.BlockSpec(memory_space=pltpu.VMEM)
    return pl.pallas_call(
        functools.partial(combine_kernel, (rows, cols, reps)),
        out_shape=jax.ShapeDtypeStruct((tokens, width), jnp.bfloat16),
        in_specs=[pl.BlockSpec(memory_space=pl.ANY), vmem, vmem],
        out_specs=vmem,
        scratch_shapes=[
            pltpu.VMEM((rows, plane, held, CAP, width), jnp.bfloat16),
            pltpu.VMEM((rows, tokens, width), jnp.bfloat16),
            pltpu.VMEM((rows, tokens, width), jnp.bfloat16),
            pltpu.VMEM((tokens, width), jnp.float32),
            pltpu.SemaphoreType.DMA((rows,)),
            pltpu.SemaphoreType.DMA((2, rows, plane)),
            pltpu.SemaphoreType.DMA((2, rows)),
        ],
        compiler_params=pltpu.CompilerParams(
            collective_id=2, has_side_effects=True, vmem_limit_bytes=VMEM_BYTES
        ),
    )(produced, tables, residual)


def token_layout(group_lengths, places):
    upto = jnp.tril(jnp.ones((group_lengths.shape[0],) * 2, jnp.int32))
    ends = jnp.sum(upto * group_lengths[None, :], axis=1)
    starts = ends - group_lengths
    member = jnp.sum((places[:, None] >= ends[None, :]).astype(jnp.int32), axis=1)
    chosen = member[:, None] == jnp.arange(group_lengths.shape[0], dtype=jnp.int32)[None, :]
    return member, places - jnp.sum(jnp.where(chosen, starts[None, :], 0), axis=1)


def slot_tables(routes, gates, planes, plane_size, per_device):
    token_count = routes.shape[0]
    experts = jnp.arange(E, dtype=jnp.int32)
    named = routes[:, :, None] == experts[None, None, :]
    chosen = jnp.sum(named.astype(jnp.float32), axis=1)
    gate = jnp.sum(jnp.where(named, gates[:, :, None], 0.0), axis=1)
    before = jnp.tril(jnp.ones((token_count, token_count), jnp.float32), -1)
    rank = jnp.dot(
        before.astype(jnp.bfloat16), chosen.astype(jnp.bfloat16), preferred_element_type=jnp.float32
    )
    slots = jnp.arange(CAP, dtype=jnp.float32)
    filled = (chosen[:, :, None] > 0) & (rank[:, :, None] == slots[None, None, :])
    tokens = jnp.arange(1, token_count + 1, dtype=jnp.float32)
    token = jnp.sum(jnp.where(filled, tokens[:, None, None], 0.0), axis=0) - 1.0
    weight = jnp.sum(jnp.where(filled, gate[:, :, None], 0.0), axis=0)
    held = max(1, per_device // 2)
    both = jnp.stack([token, weight])
    if per_device == 1:
        both = jnp.repeat(both, 2, axis=1)
    both = both.reshape(2, planes, plane_size * held * CAP).swapaxes(0, 1)
    return jnp.concatenate([both, jnp.zeros((planes, 6, both.shape[2]), jnp.float32)], axis=1)


def run_experts(rows, expert_gate_up, expert_down):
    hidden_units = expert_down.shape[1]
    outputs = []
    for half in range(expert_down.shape[0]):
        joint = jnp.dot(
            rows[half // 2], expert_gate_up[half], preferred_element_type=jnp.float32
        )
        active = (jax.nn.silu(joint[:, :hidden_units]) * joint[:, hidden_units:]).astype(
            jnp.bfloat16
        )
        outputs.append(
            jnp.dot(active, expert_down[half], preferred_element_type=jnp.float32)
            .astype(jnp.bfloat16)
            .astype(jnp.float32)
        )
    if len(outputs) == 1:
        return outputs[0][None].astype(jnp.bfloat16)
    return jnp.stack(
        [(outputs[i] + outputs[i + 1]).astype(jnp.bfloat16) for i in range(0, len(outputs), 2)]
    )


def on_device(
    hidden,
    lengths,
    prefix_latent,
    gain_in,
    query_weight,
    latent_down,
    latent_gain,
    key_absorb,
    value_up,
    output_weight,
    post_gain,
    routes,
    gate_weights,
    expert_gate_up,
    expert_down,
):
    token_count = hidden.shape[1]
    head_count = key_absorb.shape[0]
    latent_width = latent_gain.shape[0]
    scale_factor = float(query_weight.shape[1] // head_count) ** (-0.5)
    group_lengths = lengths[0]
    rows, cols, reps = (lax.axis_size(name) for name in ("row", "col", "rep"))
    prefix_total = prefix_latent.shape[0] * rows * cols * reps
    places = lax.axis_index(("row", "col")) * token_count + jnp.arange(token_count, dtype=jnp.int32)
    member, offsets = token_layout(group_lengths, places)
    own_tokens = hidden[0]
    normed = rms_scale(own_tokens.astype(jnp.float32), gain_in).astype(jnp.bfloat16)
    query_rows, key_rows = make_queries(
        normed, prefix_total + offsets, query_weight, latent_down, latent_gain, key_absorb
    )
    tables = slot_tables(
        routes[0], gate_weights[0], rows, cols * reps, expert_gate_up.shape[0]
    )
    query_rows = query_rows.reshape(token_count * head_count, -1)
    row_member = jnp.repeat(member, head_count)
    row_places = jnp.repeat(places, head_count)
    keys = gather_keys(key_rows, prefix_latent)
    block_rows = keys.shape[2]
    within = jnp.tile(jnp.arange(block_rows, dtype=jnp.int32), rows * cols)
    key_places = (
        jnp.repeat(jnp.arange(rows * cols, dtype=jnp.int32) * token_count, block_rows) + within
    )
    key_member, _ = token_layout(group_lengths, key_places)
    is_prefix = within >= token_count
    keys = keys.reshape(rows * cols * block_rows, -1)
    visible = is_prefix[None, :] | (
        (row_member[:, None] == key_member[None, :])
        & (row_places[:, None] >= key_places[None, :])
    )
    scores = (
        lax.dot_general(
            query_rows, keys, (((1,), (1,)), ((), ())), preferred_element_type=jnp.float32
        )
        * scale_factor
    )
    scores = jnp.where(visible, scores, -jnp.inf)
    weights = jnp.exp(scores - jnp.max(scores, axis=1, keepdims=True))
    normalizer = jnp.sum(weights, axis=1, keepdims=True)
    weighted = jnp.dot(
        weights.astype(jnp.bfloat16), keys[:, :latent_width], preferred_element_type=jnp.float32
    )
    mixed = (
        (weighted / normalizer).astype(jnp.bfloat16).reshape(token_count, head_count, latent_width)
    )
    head_values = (
        jnp.einsum("thr,hrv->thv", mixed, value_up, preferred_element_type=jnp.float32)
        .astype(jnp.bfloat16)
        .reshape(token_count, -1)
    )
    attention = jnp.dot(head_values, output_weight, preferred_element_type=jnp.float32)
    residual = (own_tokens.astype(jnp.float32) + attention).astype(jnp.bfloat16)
    normed_post = rms_scale(residual.astype(jnp.float32), post_gain).astype(jnp.bfloat16)
    arrived, arrived_tables = dispatch(normed_post, tables, expert_gate_up.shape[0])
    shape = arrived.shape
    produced = run_experts(
        arrived.reshape(shape[0], -1, shape[-1]), expert_gate_up, expert_down
    ).reshape(shape)
    layer_out = combine(produced, arrived_tables, residual)
    return (attention.astype(jnp.bfloat16)[None], layer_out[None])


def solution(mesh):
    in_specs = (
        P("rep", ("row", "col"), None),
        P("rep", None),
        P(("row", "col", "rep"), None),
        P(),
        P(),
        P(),
        P(),
        P(),
        P(),
        P(),
        P(),
        P("rep", ("row", "col"), None),
        P("rep", ("row", "col"), None),
        P(("row", "col", "rep"), None, None),
        P(("row", "col", "rep"), None, None),
    )
    out_specs = (P("rep", ("row", "col"), None), P("rep", ("row", "col"), None))
    return jax.shard_map(
        on_device, mesh=mesh, in_specs=in_specs, out_specs=out_specs, check_vma=False
    )
```
